256 devices in a mesh: group: 8 (over z), shard: 32 (over y, x, core).
Axes of the slice: x: 4, y: 4, z: 8, core: 2. Of those that a mesh axis runs over, the one named last changes fastest.
Arguments:
- queries: bfloat16 [8, 512, 2048], P('group', 'shard'), may hold values from -6 to 6
- fine_codebook: bfloat16 [256, 2048], replicated, may hold values from -0.125 to 0.125
- coarse_codebook: bfloat16 [256, 64], replicated, may hold values from -0.75 to 0.75
- fine_codes: int32 [64, 256, 256], P('shard'), may hold values from 0 to 255
- coarse_codes: int32 [8, 32768], P(None, 'group'), may hold values from 0 to 255
- shortlist: int32 [8, 512, 8], P('group', 'shard'), may hold values from 0 to 63, all different within a row; in each aligned block of 16 rows (0 to 15, 16 to 31, ..., all dimensions but the last counted through in order) at most 4 rows name the same one
- owner: int32 [64], replicated, may hold values from 0 to 63, each once
- block_counts: int32 [64], P('shard'), may hold values from 1 to 2
Outputs:
- coarse_scores: float32 [8, 512, 32768], P(None, 'shard', 'group')
- fine_scores: float32 [8, 512, 8, 256], P('group', 'shard')
The draws below stay inside these ranges and needn't reach their ends.
Inputs may be any that keep to these rules, and one draw needn't show every extreme that they name: `shortlist`: the 8 clusters of one query differ. Among the queries of one device (aligned blocks of 16 queries) no cluster is named by more than 4 of them, a bound that some block reaches. A permutation: cluster c is stored at slot owner[c].
All inputs are finite; a program needn't handle non-finite values.
Results may differ from the reference program's by a relative error of at most 0.0029.
Values may be sent and summed in bfloat16 or wider, within the bound.
No kernel may reach another device: no remote copies, remote signals or barrier semaphores. Data moves between devices by JAX's collectives and lax.ppermute only.
A program may use at most 128 MiB of HBM per device.

```python
import math
import jax
import jax.numpy as jnp
import numpy as np
from jax import lax

D = 2048
PREFIX = 64
MF = 256
MC = 8
K = 256
L = 8
BLOCK = 128
BMAX = 2
QD = 16
CLUSTERS = 64
MOST = 4
ROWS = 256
NSLAB = 32768
QGROUP = 512
N_GROUP = 8
N_SHARD = 32


def place_ends(array, key, smallest, largest):
    shape = array.shape
    place = [jax.random.randint(jax.random.fold_in(key, axis), (), 0, shape[axis]) for axis in range(len(shape))]
    array = array.at[tuple(place)].set(smallest)
    longest = shape.index(max(shape))
    place[longest] = (place[longest] + 1) % shape[longest]
    return array.at[tuple(place)].set(largest)


def shard_levels(stream_key, extent, shards, smallest, largest):
    def one(dim, blocks):
        steps = jax.random.uniform(jax.random.fold_in(jax.random.fold_in(stream_key, 6), dim), (blocks,), jnp.float32, smallest / len(shards), largest / len(shards))
        return jnp.repeat(jnp.exp(steps), extent[dim] // blocks).reshape((-1,) + (1,) * (len(extent) - dim - 1))

    factor_of = one(*shards[0])
    for cut in shards[1:]:
        factor_of = factor_of * one(*cut)
    return factor_of


def shared_out(key, own, number, rows, amount, top, bound, lean):
    ranking = jax.random.permutation(key, amount)
    crowded, ordinary = shares(amount, rows * top, bound, lean, True), shares(amount, rows * top, bound, lean, False)
    places = jnp.arange(amount)

    def named(tallies, turn):
        used = int((tallies > 0).sum())
        fixed = max(1, used // 4)
        passed = fixed + (places - fixed + turn * (used - fixed)) % max(1, amount - fixed)
        return jnp.zeros((amount,), jnp.int32).at[ranking[jnp.where(places < fixed, places, passed)]].set(jnp.asarray(tallies, jnp.int32))

    tallies = jnp.where(number % 4 == 0, named(crowded, number // 4), named(ordinary, number - number // 4 - 1))
    mixed = jax.random.permutation(jax.random.fold_in(own, 3), amount)
    giver, receiver = mixed[0:amount // 2 * 2:2], mixed[1:amount // 2 * 2:2]
    margin = jnp.minimum(tallies[giver] - 1, bound - tallies[receiver]) // 2
    margin = jnp.where((giver == ranking[0]) | (receiver == ranking[0]) | (tallies[receiver] == 0), 0, jnp.maximum(margin, 0))
    passed = jax.random.randint(jax.random.fold_in(own, 4), (amount // 2,), 0, 1 << 20) % (margin + 1)
    tallies = tallies.at[giver].add(-passed).at[receiver].add(passed)
    items = jnp.searchsorted(jnp.cumsum(tallies), jnp.arange(rows * top), side="right").astype(jnp.int32)
    table = items.reshape(top, rows).T
    table = table[jax.random.permutation(jax.random.fold_in(own, 1), rows)]
    turn = jax.random.randint(jax.random.fold_in(own, 2), (rows, 1), 0, top)
    return jnp.take_along_axis(table, (jnp.arange(top)[None, :] + turn) % top, axis=1)


def shares(amount, total, most, lean, full):
    portions = [(1 << 20) // math.isqrt(standing ** lean) + 1 for standing in range(1, amount + 1)]
    largest = most if full else min(most, max(-(-total // amount), total * portions[0] // sum(portions)))
    least = 1 if total - largest >= amount - 1 else 0
    counts, rest = [largest] + [least] * (amount - 1), total - largest - least * (amount - 1)
    while rest > 0:
        candidates = [i for i in range(1, amount) if counts[i] < largest] or [i for i in range(1, amount) if counts[i] < most]
        mass, remaining = sum([portions[i] for i in candidates]), rest
        for i in candidates:
            more = min(most - counts[i], max(1, remaining * portions[i] // mass), rest)
            counts[i] = counts[i] + more
            rest = rest - more
    return np.array(counts)


def scatter_about(own_key, shape, width, most, shards=(), held_as=jnp.bfloat16):
    gain = shard_levels(own_key, shape, shards, -0.22, 0.18) if shards else 1.0
    result = jax.random.normal(own_key, shape, jnp.float32) * width * gain
    return jnp.minimum(jnp.maximum(result, -most), most).astype(held_as)


def setup_inputs(seed: int = 0) -> dict:
    key_list = jax.random.split(jax.random.key(seed), 9)
    queries = scatter_about(key_list[0], (N_GROUP, QGROUP, D), 1.0, 6.0, ((0, 8), (1, 32)))
    fine_codebook = scatter_about(key_list[1], (K, D), D ** -0.5, 0.125)
    coarse_codebook = scatter_about(key_list[2], (K, PREFIX), PREFIX ** -0.5, 0.75)
    fine_codes = place_ends(jax.random.randint(key_list[3], (CLUSTERS, MF, ROWS), 0, K), jax.random.fold_in(key_list[3], 1), 0, K - 1).astype(jnp.int32)
    coarse_codes = place_ends(jax.random.randint(key_list[4], (MC, NSLAB), 0, K), jax.random.fold_in(key_list[4], 1), 0, K - 1).astype(jnp.int32)
    shortlist_keys = jax.random.split(jax.random.fold_in(key_list[5], 1), N_GROUP * QGROUP // QD)
    shortlist_turns = jax.random.permutation(jax.random.fold_in(key_list[5], 3), N_GROUP * QGROUP // QD)
    shortlist = jax.vmap(lambda own, number: shared_out(jax.random.fold_in(key_list[5], 2), own, number, QD, CLUSTERS, L, MOST, 2))(shortlist_keys, shortlist_turns).reshape((N_GROUP, QGROUP, L))
    owner = jax.random.permutation(key_list[6], CLUSTERS).astype(jnp.int32)
    block_counts = place_ends(jax.random.randint(key_list[7], (CLUSTERS,), 1, BMAX + 1), jax.random.fold_in(key_list[7], 1), 1, BMAX).astype(jnp.int32)
    return {"queries": queries, "fine_codebook": fine_codebook, "coarse_codebook": coarse_codebook, "fine_codes": fine_codes, "coarse_codes": coarse_codes, "shortlist": shortlist, "owner": owner, "block_counts": block_counts}


def lookup_tables(vector, codebook, subspaces):
    vector_width = vector.shape[0]
    stride = vector_width // subspaces
    pieces = vector.astype(jnp.float32).reshape(subspaces, stride)
    entries = codebook.astype(jnp.float32).reshape(codebook.shape[0], subspaces, stride)
    lookup = jnp.einsum("mj,kmj->mk", pieces, entries)
    return lax.optimization_barrier(lookup.astype(jnp.bfloat16)).astype(jnp.float32)


def reference(queries, fine_codebook, coarse_codebook, fine_codes, coarse_codes, shortlist, owner, block_counts):
    flat_queries = queries.reshape(-1, D)
    flat_lists = shortlist.reshape(-1, L).astype(jnp.int32)
    coarse_index = (jnp.arange(MC, dtype=jnp.int32)[:, None] * K + coarse_codes.astype(jnp.int32)).astype(jnp.int32)
    fine_index = (jnp.arange(MF, dtype=jnp.int32)[None, :, None] * K + fine_codes.astype(jnp.int32)).astype(jnp.int32)
    row_ids = jnp.arange(ROWS, dtype=jnp.int32)

    def coarse_row(vector):
        lookup = lookup_tables(vector[:PREFIX], coarse_codebook, MC)
        return jnp.sum(jnp.take(lookup.reshape(-1), coarse_index), axis=0)

    def fine_row(packed):
        vector, clusters = packed
        lookup = lookup_tables(vector, fine_codebook, MF)
        stored_at = jnp.take(owner, clusters).astype(jnp.int32)
        gathered = jnp.take(lookup.reshape(-1), jnp.take(fine_index, stored_at, axis=0))
        scores = jnp.sum(gathered, axis=1)
        row_limit = BLOCK * jnp.take(block_counts, stored_at).astype(jnp.int32)
        return jnp.where(row_ids[None, :] < row_limit[:, None], scores, jnp.zeros_like(scores))

    coarse = lax.map(coarse_row, flat_queries).reshape(N_GROUP, N_SHARD * QD, NSLAB)
    fine = lax.map(fine_row, (flat_queries, flat_lists)).reshape(N_GROUP, N_SHARD * QD, L, ROWS)
    return (coarse, fine)
```

```python
import functools

import jax
import jax.numpy as jnp
from jax import lax
from jax.experimental import pallas as pl
from jax.experimental.pallas import tpu as pltpu
from jax.sharding import PartitionSpec as P

PREFIX = 64
BLOCK = 128
CAPACITY = 4
CHUNK = 64
SPAN = 512
LANES = 128


def picked(low_half, high_half, code):
    within = code & (LANES - 1)
    from_low = jnp.take_along_axis(low_half, within, axis=1)
    from_high = jnp.take_along_axis(high_half, within, axis=1)
    return jnp.where(code < LANES, from_low, from_high)


def rebuild_pair(table, codes, first, base):
    parts = []
    for u in range(2):
        low_half = table[pl.ds(base + u * 8, 8), :LANES]
        high_half = table[pl.ds(base + u * 8, 8), LANES:]
        code = codes[first + u : first + u + 1]
        spans = []
        for r in range(0, codes.shape[1], LANES):
            index = jnp.broadcast_to(code[:, r : r + LANES], (8, LANES))
            spans.append(picked(low_half, high_half, index))
        parts.append(jnp.concatenate(spans, axis=1))
    return jnp.concatenate(parts, axis=0).astype(jnp.bfloat16)


def route_kernel(shortlist_ref, owner_ref, queries_ref, out_ref):
    lists = shortlist_ref[...]
    probes, count = lists.shape
    clusters = owner_ref.shape[1]
    ids = lax.broadcasted_iota(jnp.int32, (clusters, count), 0)
    named = jnp.zeros((clusters, count), jnp.float32)
    for entry in range(probes):
        named += (lists[entry : entry + 1, :] == ids).astype(jnp.float32)
    row = lax.broadcasted_iota(jnp.int32, (count, count), 0)
    col = lax.broadcasted_iota(jnp.int32, (count, count), 1)
    rank = jnp.dot(named, (row < col).astype(jnp.float32), preferred_element_type=jnp.float32)
    places = clusters * CAPACITY
    place = lax.broadcasted_iota(jnp.int32, (places, clusters), 0)
    stored = (owner_ref[...] == place // CAPACITY).astype(jnp.float32)
    named_at = jnp.dot(stored, named, preferred_element_type=jnp.float32)
    rank_at = jnp.dot(stored, rank, preferred_element_type=jnp.float32)
    turn = (lax.broadcasted_iota(jnp.int32, (places, count), 0) % CAPACITY).astype(jnp.float32)
    routing = jnp.where(rank_at == turn, named_at, 0.0).astype(jnp.bfloat16)
    out_ref[...] = jnp.dot(
        routing, queries_ref[...], preferred_element_type=jnp.float32
    ).astype(jnp.bfloat16)


def rebuild_kernel(codes_ref, codebook_ref, out_ref, table):
    table[...] = codebook_ref[...].astype(jnp.float32).T
    for local_id in range(codes_ref.shape[0]):

        def step(index, carry, local_id=local_id):
            first = pl.multiple_of(index * 8, 8)
            codes = codes_ref[local_id, pl.ds(first, 8), :]
            for pair in range(4):
                base = pl.multiple_of(first * 8 + pair * 16, 16)
                out_ref[local_id, pl.ds(base, 16), :] = rebuild_pair(table, codes, pair * 2, base)
            return carry

        lax.fori_loop(0, codes_ref.shape[1] // 8, step, 0, unroll=8)


def coarse_kernel(prefix_ref, codes_ref, codebook_ref, out_ref, table):
    @pl.when(pl.program_id(0) == 0)
    def _():
        table[...] = codebook_ref[...].astype(jnp.float32)

    codes = codes_ref[...]
    rebuilt = jnp.concatenate(
        [rebuild_pair(table, codes, first, first * 8) for first in range(0, codes.shape[0], 2)],
        axis=0,
    )
    out_ref[...] = jnp.dot(prefix_ref[...], rebuilt, preferred_element_type=jnp.float32)


def score_kernel(counts_ref, items_ref, rebuilt_ref, out_ref):
    local_count = rebuilt_ref.shape[0]
    rows = rebuilt_ref.shape[2]
    shape = (items_ref.shape[0], rows)
    turn = lax.broadcasted_iota(jnp.int32, shape, 0) // CAPACITY % local_count
    row_ids = lax.broadcasted_iota(jnp.int32, shape, 1)
    total = jnp.zeros(shape, jnp.float32)
    for local_id in range(local_count):
        scores = jnp.dot(
            items_ref[...], rebuilt_ref[local_id], preferred_element_type=jnp.float32
        )
        kept = (turn == local_id) & (row_ids < BLOCK * counts_ref[local_id])
        total = jnp.where(kept, scores, total)
    out_ref[...] = total


def gathered(block, axis):
    size = lax.axis_size(axis)
    place = lax.axis_index(axis)
    step = 1
    while step < size:
        other = lax.ppermute(block, axis, [(i, i ^ step) for i in range(size)])
        later = place & step != 0
        block = jnp.concatenate(
            [jnp.where(later, other, block), jnp.where(later, block, other)], axis=0
        )
        step *= 2
    return block


def body(
    queries,
    fine_codebook,
    coarse_codebook,
    fine_codes,
    coarse_codes,
    shortlist,
    owner,
    block_counts,
):
    shards = lax.axis_size("shard")
    groups = lax.axis_size("group")
    local_count, subspaces, row_count = fine_codes.shape
    per_device, width = queries.shape[1:]
    probes = shortlist.shape[2]
    clusters = owner.shape[0]
    centers = fine_codebook.shape[0]
    slab_subspaces, slab_rows = coarse_codes.shape
    positions = clusters * CAPACITY
    queries = queries[0]
    lists = shortlist[0]

    outgoing = pl.pallas_call(
        route_kernel,
        out_shape=jax.ShapeDtypeStruct((positions, width), jnp.bfloat16),
        name="route",
    )(lists.T, owner.reshape(1, clusters), queries)
    arrived = lax.all_to_all(
        outgoing.reshape(shards, positions // shards, width), "shard", 0, 0, tiled=True
    )

    prefixes = gathered(queries[:, :PREFIX], "group")

    rebuilt = pl.pallas_call(
        rebuild_kernel,
        grid=(subspaces // CHUNK,),
        in_specs=[
            pl.BlockSpec((local_count, CHUNK, row_count), lambda i: (0, i, 0)),
            pl.BlockSpec((centers, CHUNK * 8), lambda i: (0, i)),
        ],
        out_specs=pl.BlockSpec((local_count, CHUNK * 8, row_count), lambda i: (0, i, 0)),
        out_shape=jax.ShapeDtypeStruct((local_count, width, row_count), jnp.bfloat16),
        scratch_shapes=[pltpu.VMEM((CHUNK * 8, centers), jnp.float32)],
        cost_estimate=pl.CostEstimate(
            flops=4_000_000_000, bytes_accessed=4_000_000, transcendentals=0
        ),
        name="rebuild",
    )(fine_codes, fine_codebook)

    coarse_scores = pl.pallas_call(
        coarse_kernel,
        grid=(slab_rows // SPAN,),
        in_specs=[
            pl.BlockSpec((groups * per_device, PREFIX), lambda i: (0, 0)),
            pl.BlockSpec((slab_subspaces, SPAN), lambda i: (0, i)),
            pl.BlockSpec((PREFIX, centers), lambda i: (0, 0)),
        ],
        out_specs=pl.BlockSpec((groups * per_device, SPAN), lambda i: (0, i)),
        out_shape=jax.ShapeDtypeStruct((groups * per_device, slab_rows), jnp.float32),
        scratch_shapes=[pltpu.VMEM((PREFIX, centers), jnp.float32)],
        cost_estimate=pl.CostEstimate(
            flops=2_000_000_000, bytes_accessed=4_000_000, transcendentals=0
        ),
        name="coarse",
    )(prefixes, coarse_codes, coarse_codebook.T)

    computed = pl.pallas_call(
        score_kernel,
        in_specs=[
            pl.BlockSpec(memory_space=pltpu.SMEM),
            pl.BlockSpec(memory_space=pltpu.VMEM),
            pl.BlockSpec(memory_space=pltpu.VMEM),
        ],
        out_shape=jax.ShapeDtypeStruct((positions, row_count), jnp.float32),
        name="score",
    )(block_counts, arrived.reshape(positions, width), rebuilt)
    returned = lax.all_to_all(
        computed.reshape(shards, positions // shards, row_count), "shard", 0, 0, tiled=True
    ).reshape(positions, row_count)

    flat = lists.reshape(-1)
    storage = jnp.sum(
        jnp.where(flat[:, None] == jnp.arange(clusters)[None, :], owner[None, :], 0), axis=1
    )
    items = jnp.arange(flat.shape[0])
    earlier = (flat[:, None] == flat[None, :]) & (items[:, None] > items[None, :])
    target = storage * CAPACITY + jnp.sum(earlier.astype(jnp.int32), axis=1)
    fine_scores = jnp.take(returned, target, axis=0)
    return (
        coarse_scores.reshape(groups, per_device, slab_rows),
        fine_scores.reshape(1, per_device, probes, row_count),
    )


def solution(mesh):
    in_specs = (
        P("group", "shard", None),
        P(),
        P(),
        P("shard", None, None),
        P(None, "group"),
        P("group", "shard", None),
        P(),
        P("shard"),
    )
    out_specs = (P(None, "shard", "group"), P("group", "shard", None, None))
    return jax.shard_map(body, mesh=mesh, in_specs=in_specs, out_specs=out_specs, check_vma=False)
```

```python
import functools

import jax
import jax.numpy as jnp
from jax import lax
from jax.experimental import pallas as pl
from jax.experimental.pallas import tpu as pltpu
from jax.sharding import PartitionSpec as P

PREFIX = 64
BLOCK = 128
CAPACITY = 4
CHUNK = 64
SPAN = 2048
LANES = 128


def looked_up(halves, code):
    within = code & (LANES - 1)
    low = code < LANES
    found = [
        (jnp.take_along_axis(first, within, axis=1), jnp.take_along_axis(last, within, axis=1))
        for first, last in halves
    ]
    columns = [jnp.where(low, first, last) for first, last in found]
    return [
        jnp.concatenate(columns[j : j + 2], axis=0).astype(jnp.bfloat16)
        for j in range(0, len(columns), 2)
    ]


def table_rows(table, base):
    return [
        tuple(table[half, pl.ds(base + j, 8, stride=8), :] for half in range(2)) for j in range(8)
    ]


def fill_table(table, columns):
    table[0] = columns[:, :LANES]
    table[1] = columns[:, LANES:]


def route_kernel(owner_lanes, owner_ref, lists_ref, queries_ref, out_ref, prefix_ref, place_ref):
    lists = lists_ref[...]
    probes, count = lists.shape
    width = queries_ref.shape[1]
    clusters = owner_ref.shape[0]
    places = clusters * CAPACITY
    ids = lax.broadcasted_iota(jnp.int32, (clusters, count), 0)
    names = [lists[entry : entry + 1, :] == ids for entry in range(probes)]
    named = sum(name.astype(jnp.float32) for name in names)
    before = lax.broadcasted_iota(jnp.int32, (count, count), 0)
    after = lax.broadcasted_iota(jnp.int32, (count, count), 1)
    rank = jnp.dot(named, (before < after).astype(jnp.float32), preferred_element_type=jnp.float32)
    place = lax.broadcasted_iota(jnp.int32, (places, clusters), 0)
    stored = (owner_lanes[...] == place // CAPACITY).astype(jnp.float32)
    named_at = jnp.dot(stored, named, preferred_element_type=jnp.float32)
    rank_at = jnp.dot(stored, rank, preferred_element_type=jnp.float32)
    turn = (lax.broadcasted_iota(jnp.int32, (places, count), 0) % CAPACITY).astype(jnp.float32)
    routing = jnp.where(rank_at == turn, named_at, 0.0).astype(jnp.bfloat16)
    lane = lax.broadcasted_iota(jnp.int32, (count, LANES), 1)
    source = lane // 64 * 64 + lane % 8 * 8 + lane // 8 % 8
    for first in range(0, width, LANES):
        piece = queries_ref[:, first : first + LANES].astype(jnp.float32)
        piece = jnp.take_along_axis(piece, source, axis=1).astype(jnp.bfloat16)
        out_ref[:, first : first + LANES] = jnp.dot(
            routing, piece, preferred_element_type=jnp.float32
        ).astype(jnp.bfloat16)
        if first == 0:
            prefix_ref[...] = piece[:, :PREFIX]
    slots = jnp.zeros(lists.shape, jnp.int32)
    for cluster in range(clusters):
        slots = jnp.where(lists == cluster, owner_ref[cluster], slots)
    ranks = jnp.concatenate(
        [jnp.sum(jnp.where(name, rank, 0.0), axis=0, keepdims=True) for name in names], axis=0
    )
    target = (slots * CAPACITY).astype(jnp.float32) + ranks
    items = count * probes
    row = lax.broadcasted_iota(jnp.int32, (items, probes), 0)
    entry = lax.broadcasted_iota(jnp.int32, (items, probes), 1)
    pick = (row % probes == entry).astype(jnp.float32)
    spread = jnp.dot(pick, target, preferred_element_type=jnp.float32)
    row = lax.broadcasted_iota(jnp.int32, (items, count), 0)
    query = lax.broadcasted_iota(jnp.int32, (items, count), 1)
    target = jnp.sum(jnp.where(row // probes == query, spread, 0.0), axis=1, keepdims=True)
    place = lax.broadcasted_iota(jnp.int32, place_ref.shape, 1)
    place_ref[...] = (place == target.astype(jnp.int32)).astype(jnp.float32)


def rebuild_kernel(counts_ref, codes_ref, codebook_ref, first_ref, second_ref, table):
    fill_table(table, codebook_ref[...].astype(jnp.float32).T)

    def step(index, carry):
        first = pl.multiple_of(index * 8, 8)
        base = pl.multiple_of(index * 64, 64)
        halves = table_rows(table, base)
        for local_id, out_ref in enumerate((first_ref, second_ref)):
            for start in range(0, codes_ref.shape[2], LANES):
                codes = codes_ref[local_id, pl.ds(first, 8), start : start + LANES]
                filled = start < BLOCK * counts_ref[local_id]
                for number, tile in enumerate(looked_up(halves, codes)):
                    out_ref[pl.ds(base + number * 16, 16), start : start + LANES] = jnp.where(
                        filled, tile, jnp.zeros_like(tile)
                    )
        return carry

    lax.fori_loop(0, codes_ref.shape[1] // 8, step, 0, unroll=True)


def coarse_kernel(prefix_ref, codes_ref, codebook_ref, out_ref, table, rebuilt):
    @pl.when(pl.program_id(0) == 0)
    def _():
        fill_table(table, codebook_ref[...].astype(jnp.float32))

    halves = table_rows(table, 0)
    for start in range(0, codes_ref.shape[1], LANES):
        tiles = looked_up(halves, codes_ref[:, start : start + LANES])
        for number, tile in enumerate(tiles):
            rebuilt[number * 16 : number * 16 + 16, start : start + LANES] = tile
    out_ref[...] = jnp.dot(prefix_ref[...], rebuilt[...], preferred_element_type=jnp.float32)


def body(
    queries,
    fine_codebook,
    coarse_codebook,
    fine_codes,
    coarse_codes,
    shortlist,
    owner,
    block_counts,
):
    shards = lax.axis_size("shard")
    groups = lax.axis_size("group")
    local_count, subspaces, row_count = fine_codes.shape
    per_device, width = queries.shape[1:]
    probes = shortlist.shape[2]
    clusters = owner.shape[0]
    centers = fine_codebook.shape[0]
    slab_subspaces, slab_rows = coarse_codes.shape
    positions = clusters * CAPACITY
    queries = queries[0]
    lists = shortlist[0]

    whole = pl.BlockSpec(memory_space=pltpu.VMEM)
    outgoing, prefix, place = pl.pallas_call(
        route_kernel,
        in_specs=[whole, pl.BlockSpec(memory_space=pltpu.SMEM), whole, whole],
        out_shape=[
            jax.ShapeDtypeStruct((positions, width), jnp.bfloat16),
            jax.ShapeDtypeStruct((per_device, PREFIX), jnp.bfloat16),
            jax.ShapeDtypeStruct((per_device * probes, positions), jnp.float32),
        ],
        name="route",
    )(owner.reshape(1, clusters), owner, lists.T, queries)
    arrived = lax.all_to_all(
        outgoing.reshape(shards, positions // shards, width), "shard", 0, 0, tiled=True
    ).reshape(positions, width)

    span = CHUNK * (width // subspaces)
    rebuilt_block = pl.BlockSpec((span, row_count), lambda i: (i, 0))
    rebuilt_shape = jax.ShapeDtypeStruct((width, row_count), jnp.bfloat16)
    rebuilt = pl.pallas_call(
        rebuild_kernel,
        grid=(subspaces // CHUNK,),
        in_specs=[
            pl.BlockSpec(memory_space=pltpu.SMEM),
            pl.BlockSpec((local_count, CHUNK, row_count), lambda i: (0, i, 0)),
            pl.BlockSpec((centers, span), lambda i: (0, i)),
        ],
        out_specs=[rebuilt_block, rebuilt_block],
        out_shape=[rebuilt_shape, rebuilt_shape],
        scratch_shapes=[pltpu.VMEM((2, span, LANES), jnp.float32)],
        cost_estimate=pl.CostEstimate(
            flops=1_000_000, bytes_accessed=100_000, transcendentals=0
        ),
        name="rebuild",
    )(block_counts, fine_codes, fine_codebook)

    def from_group(value, offset):
        pairs = [((i + offset) % groups, i) for i in range(groups)]
        return lax.ppermute(value, "group", pairs)

    near = jnp.concatenate([from_group(prefix, -1), prefix, from_group(prefix, 1)], axis=0)
    around = jnp.concatenate(
        [from_group(near, -3), near, from_group(near[: 2 * per_device], 3)], axis=0
    ).reshape(groups, per_device, PREFIX)
    first = lax.axis_index("group") + groups // 2
    prefixes = jnp.roll(around, first, axis=0).reshape(groups * per_device, PREFIX)
    coarse_scores = pl.pallas_call(
        coarse_kernel,
        grid=(slab_rows // SPAN,),
        in_specs=[
            pl.BlockSpec((groups * per_device, PREFIX), lambda i: (0, 0)),
            pl.BlockSpec((slab_subspaces, SPAN), lambda i: (0, i)),
            pl.BlockSpec((PREFIX, centers), lambda i: (0, 0)),
        ],
        out_specs=pl.BlockSpec((groups * per_device, SPAN), lambda i: (0, i)),
        out_shape=jax.ShapeDtypeStruct((groups * per_device, slab_rows), jnp.float32),
        scratch_shapes=[
            pltpu.VMEM((2, PREFIX, LANES), jnp.float32),
            pltpu.VMEM((PREFIX, SPAN), jnp.bfloat16),
        ],
        cost_estimate=pl.CostEstimate(
            flops=1_000_000, bytes_accessed=100_000, transcendentals=0
        ),
        name="coarse",
    )(prefixes, coarse_codes, coarse_codebook.T)

    scores = [
        jnp.dot(arrived, columns, preferred_element_type=jnp.float32) for columns in rebuilt
    ]
    local = (jnp.arange(positions) // CAPACITY % local_count)[:, None]
    computed = jnp.where(local == 0, scores[0], scores[1])
    returned = lax.all_to_all(
        computed.reshape(shards, positions // shards, row_count), "shard", 0, 0, tiled=True
    ).reshape(positions, row_count)
    fine_scores = jnp.dot(
        place, returned, precision=lax.Precision.HIGHEST, preferred_element_type=jnp.float32
    )
    return (
        coarse_scores.reshape(groups, per_device, slab_rows),
        fine_scores.reshape(1, per_device, probes, row_count),
    )


def solution(mesh):
    in_specs = (
        P("group", "shard", None),
        P(),
        P(),
        P("shard", None, None),
        P(None, "group"),
        P("group", "shard", None),
        P(),
        P("shard"),
    )
    out_specs = (P(None, "shard", "group"), P("group", "shard", None, None))
    return jax.shard_map(body, mesh=mesh, in_specs=in_specs, out_specs=out_specs, check_vma=False)
```

```python
import functools

import jax
import jax.numpy as jnp
from jax import lax
from jax.experimental import pallas as pl
from jax.experimental.pallas import tpu as pltpu
from jax.sharding import PartitionSpec as P

PREFIX = 64
BLOCK = 128
CAPACITY = 4
CHUNK = 64
SPAN = 2048
LANES = 128


def looked_up(halves, code):
    within = code & (LANES - 1)
    low = code < LANES
    found = [
        (jnp.take_along_axis(first, within, axis=1), jnp.take_along_axis(last, within, axis=1))
        for first, last in halves
    ]
    columns = [jnp.where(low, first, last) for first, last in found]
    return [
        jnp.concatenate(columns[j : j + 2], axis=0).astype(jnp.bfloat16)
        for j in range(0, len(columns), 2)
    ]


def table_rows(table, base):
    return [
        tuple(table[half, pl.ds(base + j, 8, stride=8), :] for half in range(2)) for j in range(8)
    ]


def fill_table(table, columns):
    table[0] = columns[:, :LANES]
    table[1] = columns[:, LANES:]


def route_kernel(owner_lanes, owner_ref, lists_ref, queries_ref, out_ref, prefix_ref, place_ref):
    lists = lists_ref[...]
    probes, count = lists.shape
    width = queries_ref.shape[1]
    clusters = owner_ref.shape[0]
    places = clusters * CAPACITY
    ids = lax.broadcasted_iota(jnp.int32, (clusters, count), 0)
    names = [lists[entry : entry + 1, :] == ids for entry in range(probes)]
    named = sum(name.astype(jnp.float32) for name in names)
    before = lax.broadcasted_iota(jnp.int32, (count, count), 0)
    after = lax.broadcasted_iota(jnp.int32, (count, count), 1)
    rank = jnp.dot(named, (before < after).astype(jnp.float32), preferred_element_type=jnp.float32)
    place = lax.broadcasted_iota(jnp.int32, (places, clusters), 0)
    stored = (owner_lanes[...] == place // CAPACITY).astype(jnp.float32)
    named_at = jnp.dot(stored, named, preferred_element_type=jnp.float32)
    rank_at = jnp.dot(stored, rank, preferred_element_type=jnp.float32)
    turn = (lax.broadcasted_iota(jnp.int32, (places, count), 0) % CAPACITY).astype(jnp.float32)
    routing = jnp.where(rank_at == turn, named_at, 0.0).astype(jnp.bfloat16)
    lane = lax.broadcasted_iota(jnp.int32, (count, LANES), 1)
    source = lane // 64 * 64 + lane % 8 * 8 + lane // 8 % 8
    for first in range(0, width, LANES):
        piece = queries_ref[:, first : first + LANES].astype(jnp.float32)
        piece = jnp.take_along_axis(piece, source, axis=1).astype(jnp.bfloat16)
        out_ref[:, first : first + LANES] = jnp.dot(
            routing, piece, preferred_element_type=jnp.float32
        ).astype(jnp.bfloat16)
        if first == 0:
            prefix_ref[...] = piece[:, :PREFIX]
    slots = jnp.zeros(lists.shape, jnp.int32)
    for cluster in range(clusters):
        slots = jnp.where(lists == cluster, owner_ref[cluster], slots)
    ranks = jnp.concatenate(
        [jnp.sum(jnp.where(name, rank, 0.0), axis=0, keepdims=True) for name in names], axis=0
    )
    target = (slots * CAPACITY).astype(jnp.float32) + ranks
    items = count * probes
    row = lax.broadcasted_iota(jnp.int32, (items, probes), 0)
    entry = lax.broadcasted_iota(jnp.int32, (items, probes), 1)
    pick = (row % probes == entry).astype(jnp.float32)
    spread = jnp.dot(pick, target, preferred_element_type=jnp.float32)
    row = lax.broadcasted_iota(jnp.int32, (items, count), 0)
    query = lax.broadcasted_iota(jnp.int32, (items, count), 1)
    target = jnp.sum(jnp.where(row // probes == query, spread, 0.0), axis=1, keepdims=True)
    place = lax.broadcasted_iota(jnp.int32, place_ref.shape, 1)
    place_ref[...] = (place == target.astype(jnp.int32)).astype(jnp.float32)


def rebuild_kernel(counts_ref, codes_ref, codebook_ref, first_ref, second_ref, table):
    fill_table(table, codebook_ref[...].astype(jnp.float32).T)

    def step(index, carry):
        first = pl.multiple_of(index * 8, 8)
        base = pl.multiple_of(index * 64, 64)
        halves = table_rows(table, base)
        for local_id, out_ref in enumerate((first_ref, second_ref)):
            for start in range(0, codes_ref.shape[2], LANES):
                codes = codes_ref[local_id, pl.ds(first, 8), start : start + LANES]
                filled = start < BLOCK * counts_ref[local_id]
                for number, tile in enumerate(looked_up(halves, codes)):
                    out_ref[pl.ds(base + number * 16, 16), start : start + LANES] = jnp.where(
                        filled, tile, jnp.zeros_like(tile)
                    )
        return carry

    lax.fori_loop(0, codes_ref.shape[1] // 8, step, 0, unroll=True)


def coarse_kernel(prefix_ref, codes_ref, codebook_ref, out_ref, table, rebuilt):
    @pl.when(pl.program_id(0) == 0)
    def _():
        fill_table(table, codebook_ref[...].astype(jnp.float32))

    halves = table_rows(table, 0)
    for start in range(0, codes_ref.shape[1], LANES):
        tiles = looked_up(halves, codes_ref[:, start : start + LANES])
        for number, tile in enumerate(tiles):
            rebuilt[number * 16 : number * 16 + 16, start : start + LANES] = tile
    out_ref[...] = jnp.dot(prefix_ref[...], rebuilt[...], preferred_element_type=jnp.float32)


def body(
    queries,
    fine_codebook,
    coarse_codebook,
    fine_codes,
    coarse_codes,
    shortlist,
    owner,
    block_counts,
):
    shards = lax.axis_size("shard")
    groups = lax.axis_size("group")
    local_count, subspaces, row_count = fine_codes.shape
    per_device, width = queries.shape[1:]
    probes = shortlist.shape[2]
    clusters = owner.shape[0]
    centers = fine_codebook.shape[0]
    slab_subspaces, slab_rows = coarse_codes.shape
    positions = clusters * CAPACITY
    queries = queries[0]
    lists = shortlist[0]

    whole = pl.BlockSpec(memory_space=pltpu.VMEM)
    outgoing, prefix, place = pl.pallas_call(
        route_kernel,
        in_specs=[whole, pl.BlockSpec(memory_space=pltpu.SMEM), whole, whole],
        out_shape=[
            jax.ShapeDtypeStruct((positions, width), jnp.bfloat16),
            jax.ShapeDtypeStruct((per_device, PREFIX), jnp.bfloat16),
            jax.ShapeDtypeStruct((per_device * probes, positions), jnp.float32),
        ],
        name="route",
    )(owner.reshape(1, clusters), owner, lists.T, queries)
    arrived = lax.all_to_all(
        outgoing.reshape(shards, positions // shards, width), "shard", 0, 0, tiled=True
    ).reshape(positions, width)

    span = CHUNK * (width // subspaces)
    rebuilt_block = pl.BlockSpec((span, row_count), lambda i: (i, 0))
    rebuilt_shape = jax.ShapeDtypeStruct((width, row_count), jnp.bfloat16)
    rebuilt = pl.pallas_call(
        rebuild_kernel,
        grid=(subspaces // CHUNK,),
        in_specs=[
            pl.BlockSpec(memory_space=pltpu.SMEM),
            pl.BlockSpec((local_count, CHUNK, row_count), lambda i: (0, i, 0)),
            pl.BlockSpec((centers, span), lambda i: (0, i)),
        ],
        out_specs=[rebuilt_block, rebuilt_block],
        out_shape=[rebuilt_shape, rebuilt_shape],
        scratch_shapes=[pltpu.VMEM((2, span, LANES), jnp.float32)],
        cost_estimate=pl.CostEstimate(
            flops=1_000_000, bytes_accessed=100_000, transcendentals=0
        ),
        name="rebuild",
    )(block_counts, fine_codes, fine_codebook)

    def from_group(value, offset):
        pairs = [((i + offset) % groups, i) for i in range(groups)]
        return lax.ppermute(value, "group", pairs)

    near = jnp.concatenate([from_group(prefix, -1), prefix, from_group(prefix, 1)], axis=0)
    around = jnp.concatenate(
        [from_group(near, -3), near, from_group(near[: 2 * per_device], 3)], axis=0
    ).reshape(groups, per_device, PREFIX)
    first = lax.axis_index("group") + groups // 2
    prefixes = jnp.roll(around, first, axis=0).reshape(groups * per_device, PREFIX)
    coarse_scores = pl.pallas_call(
        coarse_kernel,
        grid=(slab_rows // SPAN,),
        in_specs=[
            pl.BlockSpec((groups * per_device, PREFIX), lambda i: (0, 0)),
            pl.BlockSpec((slab_subspaces, SPAN), lambda i: (0, i)),
            pl.BlockSpec((PREFIX, centers), lambda i: (0, 0)),
        ],
        out_specs=pl.BlockSpec((groups * per_device, SPAN), lambda i: (0, i)),
        out_shape=jax.ShapeDtypeStruct((groups * per_device, slab_rows), jnp.float32),
        scratch_shapes=[
            pltpu.VMEM((2, PREFIX, LANES), jnp.float32),
            pltpu.VMEM((PREFIX, SPAN), jnp.bfloat16),
        ],
        cost_estimate=pl.CostEstimate(
            flops=1_000_000, bytes_accessed=100_000, transcendentals=0
        ),
        name="coarse",
    )(prefixes, coarse_codes, coarse_codebook.T)

    scores = [
        jnp.dot(arrived, columns, preferred_element_type=jnp.float32) for columns in rebuilt
    ]
    local = (jnp.arange(positions) // CAPACITY % local_count)[:, None]
    computed = jnp.where(local == 0, scores[0], scores[1])
    computed = computed.astype(jnp.bfloat16)
    returned = lax.all_to_all(
        computed.reshape(shards, positions // shards, row_count), "shard", 0, 0, tiled=True
    ).reshape(positions, row_count)
    fine_scores = jnp.dot(
        place.astype(jnp.bfloat16), returned, preferred_element_type=jnp.float32
    )
    return (
        coarse_scores.reshape(groups, per_device, slab_rows),
        fine_scores.reshape(1, per_device, probes, row_count),
    )


def solution(mesh):
    in_specs = (
        P("group", "shard", None),
        P(),
        P(),
        P("shard", None, None),
        P(None, "group"),
        P("group", "shard", None),
        P(),
        P("shard"),
    )
    out_specs = (P(None, "shard", "group"), P("group", "shard", None, None))
    return jax.shard_map(body, mesh=mesh, in_specs=in_specs, out_specs=out_specs, check_vma=False)
```

```python
import functools

import jax
import jax.numpy as jnp
from jax import lax
from jax.experimental import pallas as pl
from jax.experimental.pallas import tpu as pltpu
from jax.sharding import PartitionSpec as P

PREFIX = 64
BLOCK = 128
CAPACITY = 4
CHUNK = 128
SPAN = 2048
LANES = 128


def looked_up(halves, code):
    within = code & (LANES - 1)
    low = code < LANES
    found = [
        (jnp.take_along_axis(first, within, axis=1), jnp.take_along_axis(last, within, axis=1))
        for first, last in halves
    ]
    columns = [jnp.where(low, first, last) for first, last in found]
    return [
        jnp.concatenate(columns[j : j + 2], axis=0).astype(jnp.bfloat16)
        for j in range(0, len(columns), 2)
    ]


def table_rows(table, base):
    return [
        tuple(table[half, pl.ds(base + j, 8, stride=8), :] for half in range(2)) for j in range(8)
    ]


def fill_table(table, columns):
    table[0] = columns[:, :LANES]
    table[1] = columns[:, LANES:]


def route_kernel(owner_lanes, owner_ref, lists_ref, queries_ref, out_ref, prefix_ref, place_ref):
    lists = lists_ref[...]
    probes, count = lists.shape
    width = queries_ref.shape[1]
    clusters = owner_ref.shape[0]
    places = clusters * CAPACITY
    ids = lax.broadcasted_iota(jnp.int32, (clusters, count), 0)
    names = [lists[entry : entry + 1, :] == ids for entry in range(probes)]
    named = sum(name.astype(jnp.float32) for name in names)
    before = lax.broadcasted_iota(jnp.int32, (count, count), 0)
    after = lax.broadcasted_iota(jnp.int32, (count, count), 1)
    rank = jnp.dot(named, (before < after).astype(jnp.float32), preferred_element_type=jnp.float32)
    place = lax.broadcasted_iota(jnp.int32, (places, clusters), 0)
    stored = (owner_lanes[...] == place // CAPACITY).astype(jnp.float32)
    named_at = jnp.dot(stored, named, preferred_element_type=jnp.float32)
    rank_at = jnp.dot(stored, rank, preferred_element_type=jnp.float32)
    turn = (lax.broadcasted_iota(jnp.int32, (places, count), 0) % CAPACITY).astype(jnp.float32)
    routing = jnp.where(rank_at == turn, named_at, 0.0).astype(jnp.bfloat16)
    lane = lax.broadcasted_iota(jnp.int32, (count, LANES), 1)
    source = lane // 64 * 64 + lane % 8 * 8 + lane // 8 % 8
    for first in range(0, width, LANES):
        piece = queries_ref[:, first : first + LANES].astype(jnp.float32)
        piece = jnp.take_along_axis(piece, source, axis=1).astype(jnp.bfloat16)
        out_ref[:, first : first + LANES] = jnp.dot(
            routing, piece, preferred_element_type=jnp.float32
        ).astype(jnp.bfloat16)
        if first == 0:
            prefix_ref[...] = piece[:, :PREFIX]
    slots = jnp.zeros(lists.shape, jnp.int32)
    for cluster in range(clusters):
        slots = jnp.where(lists == cluster, owner_ref[cluster], slots)
    ranks = jnp.concatenate(
        [jnp.sum(jnp.where(name, rank, 0.0), axis=0, keepdims=True) for name in names], axis=0
    )
    target = (slots * CAPACITY).astype(jnp.float32) + ranks
    items = count * probes
    row = lax.broadcasted_iota(jnp.int32, (items, probes), 0)
    entry = lax.broadcasted_iota(jnp.int32, (items, probes), 1)
    pick = (row % probes == entry).astype(jnp.float32)
    spread = jnp.dot(pick, target, preferred_element_type=jnp.float32)
    row = lax.broadcasted_iota(jnp.int32, (items, count), 0)
    query = lax.broadcasted_iota(jnp.int32, (items, count), 1)
    target = jnp.sum(jnp.where(row // probes == query, spread, 0.0), axis=1, keepdims=True)
    place = lax.broadcasted_iota(jnp.int32, place_ref.shape, 1)
    place_ref[...] = (place == target.astype(jnp.int32)).astype(jnp.float32)


def rebuild_kernel(counts_ref, codes_ref, codebook_ref, first_ref, second_ref, table):
    fill_table(table, codebook_ref[...].T.astype(jnp.float32))

    def step(index, carry):
        first = pl.multiple_of(index * 8, 8)
        base = pl.multiple_of(index * 64, 64)
        halves = table_rows(table, base)
        for local_id, out_ref in enumerate((first_ref, second_ref)):
            for start in range(0, codes_ref.shape[2], LANES):
                codes = codes_ref[local_id, pl.ds(first, 8), start : start + LANES]
                filled = start < BLOCK * counts_ref[local_id]
                for number, tile in enumerate(looked_up(halves, codes)):
                    out_ref[pl.ds(base + number * 16, 16), start : start + LANES] = jnp.where(
                        filled, tile, jnp.zeros_like(tile)
                    )
        return carry

    lax.fori_loop(0, codes_ref.shape[1] // 8, step, 0, unroll=True)


def coarse_kernel(prefix_ref, codes_ref, codebook_ref, out_ref, table, rebuilt):
    @pl.when(pl.program_id(0) == 0)
    def _():
        fill_table(table, codebook_ref[...].astype(jnp.float32))

    halves = table_rows(table, 0)
    for start in range(0, codes_ref.shape[1], LANES):
        tiles = looked_up(halves, codes_ref[:, start : start + LANES])
        for number, tile in enumerate(tiles):
            rebuilt[number * 16 : number * 16 + 16, start : start + LANES] = tile
    out_ref[...] = jnp.dot(prefix_ref[...], rebuilt[...], preferred_element_type=jnp.float32)


def body(
    queries,
    fine_codebook,
    coarse_codebook,
    fine_codes,
    coarse_codes,
    shortlist,
    owner,
    block_counts,
):
    shards = lax.axis_size("shard")
    groups = lax.axis_size("group")
    local_count, subspaces, row_count = fine_codes.shape
    per_device, width = queries.shape[1:]
    probes = shortlist.shape[2]
    clusters = owner.shape[0]
    centers = fine_codebook.shape[0]
    slab_subspaces, slab_rows = coarse_codes.shape
    positions = clusters * CAPACITY
    queries = queries[0]
    lists = shortlist[0]

    whole = pl.BlockSpec(memory_space=pltpu.VMEM)
    outgoing, prefix, place = pl.pallas_call(
        route_kernel,
        in_specs=[whole, pl.BlockSpec(memory_space=pltpu.SMEM), whole, whole],
        out_shape=[
            jax.ShapeDtypeStruct((positions, width), jnp.bfloat16),
            jax.ShapeDtypeStruct((per_device, PREFIX), jnp.bfloat16),
            jax.ShapeDtypeStruct((per_device * probes, positions), jnp.float32),
        ],
        name="route",
    )(owner.reshape(1, clusters), owner, lists.T, queries)
    arrived = lax.all_to_all(
        outgoing.reshape(shards, positions // shards, width), "shard", 0, 0, tiled=True
    ).reshape(positions, width)

    span = CHUNK * (width // subspaces)
    rebuilt_block = pl.BlockSpec((span, row_count), lambda i: (i, 0))
    rebuilt_shape = jax.ShapeDtypeStruct((width, row_count), jnp.bfloat16)
    rebuilt = pl.pallas_call(
        rebuild_kernel,
        grid=(subspaces // CHUNK,),
        in_specs=[
            pl.BlockSpec(memory_space=pltpu.SMEM),
            pl.BlockSpec((local_count, CHUNK, row_count), lambda i: (0, i, 0)),
            pl.BlockSpec((centers, span), lambda i: (0, i)),
        ],
        out_specs=[rebuilt_block, rebuilt_block],
        out_shape=[rebuilt_shape, rebuilt_shape],
        scratch_shapes=[pltpu.VMEM((2, span, LANES), jnp.float32)],
        cost_estimate=pl.CostEstimate(
            flops=1_000_000, bytes_accessed=100_000, transcendentals=0
        ),
        name="rebuild",
    )(block_counts, fine_codes, fine_codebook)

    def from_group(value, offset):
        pairs = [((i + offset) % groups, i) for i in range(groups)]
        return lax.ppermute(value, "group", pairs)

    near = jnp.concatenate([from_group(prefix, -1), prefix, from_group(prefix, 1)], axis=0)
    around = jnp.concatenate(
        [from_group(near, -3), near, from_group(near[: 2 * per_device], 3)], axis=0
    ).reshape(groups, per_device, PREFIX)
    first = lax.axis_index("group") + groups // 2
    prefixes = jnp.roll(around, first, axis=0).reshape(groups * per_device, PREFIX)
    coarse_scores = pl.pallas_call(
        coarse_kernel,
        grid=(slab_rows // SPAN,),
        in_specs=[
            pl.BlockSpec((groups * per_device, PREFIX), lambda i: (0, 0)),
            pl.BlockSpec((slab_subspaces, SPAN), lambda i: (0, i)),
            pl.BlockSpec((PREFIX, centers), lambda i: (0, 0)),
        ],
        out_specs=pl.BlockSpec((groups * per_device, SPAN), lambda i: (0, i)),
        out_shape=jax.ShapeDtypeStruct((groups * per_device, slab_rows), jnp.float32),
        scratch_shapes=[
            pltpu.VMEM((2, PREFIX, LANES), jnp.float32),
            pltpu.VMEM((PREFIX, SPAN), jnp.bfloat16),
        ],
        cost_estimate=pl.CostEstimate(
            flops=1_000_000, bytes_accessed=100_000, transcendentals=0
        ),
        name="coarse",
    )(prefixes, coarse_codes, coarse_codebook.T)

    scores = [
        jnp.dot(arrived, columns, preferred_element_type=jnp.float32) for columns in rebuilt
    ]
    local = (jnp.arange(positions) // CAPACITY % local_count)[:, None]
    computed = jnp.where(local == 0, scores[0], scores[1])
    computed = computed.astype(jnp.bfloat16)
    returned = lax.all_to_all(
        computed.reshape(shards, positions // shards, row_count), "shard", 0, 0, tiled=True
    ).reshape(positions, row_count)
    fine_scores = jnp.dot(
        place.astype(jnp.bfloat16), returned, preferred_element_type=jnp.float32
    )
    return (
        coarse_scores.reshape(groups, per_device, slab_rows),
        fine_scores.reshape(1, per_device, probes, row_count),
    )


def solution(mesh):
    in_specs = (
        P("group", "shard", None),
        P(),
        P(),
        P("shard", None, None),
        P(None, "group"),
        P("group", "shard", None),
        P(),
        P("shard"),
    )
    out_specs = (P(None, "shard", "group"), P("group", "shard", None, None))
    return jax.shard_map(body, mesh=mesh, in_specs=in_specs, out_specs=out_specs, check_vma=False)
```

```python
import functools

import jax
import jax.numpy as jnp
from jax import lax
from jax.experimental import pallas as pl
from jax.experimental.pallas import tpu as pltpu
from jax.sharding import PartitionSpec as P

PREFIX = 64
BLOCK = 128
CAPACITY = 4
CHUNK = 128
SPAN = 2048
LANES = 128


def looked_up(halves, code):
    within = code & (LANES - 1)
    low = code < LANES
    found = [
        (jnp.take_along_axis(first, within, axis=1), jnp.take_along_axis(last, within, axis=1))
        for first, last in halves
    ]
    columns = [jnp.where(low, first, last) for first, last in found]
    return [
        jnp.concatenate(columns[j : j + 2], axis=0).astype(jnp.bfloat16)
        for j in range(0, len(columns), 2)
    ]


def table_rows(table, base):
    return [
        tuple(table[half, pl.ds(base + j, 8, stride=8), :] for half in range(2)) for j in range(8)
    ]


def fill_table(table, columns):
    table[0] = columns[:, :LANES]
    table[1] = columns[:, LANES:]


def route_kernel(owner_lanes, owner_ref, lists_ref, queries_ref, out_ref, prefix_ref, place_ref):
    lists = lists_ref[...]
    probes, count = lists.shape
    width = queries_ref.shape[1]
    clusters = owner_ref.shape[0]
    places = clusters * CAPACITY
    ids = lax.broadcasted_iota(jnp.int32, (clusters, count), 0)
    names = [lists[entry : entry + 1, :] == ids for entry in range(probes)]
    named = sum(name.astype(jnp.float32) for name in names)
    before = lax.broadcasted_iota(jnp.int32, (count, count), 0)
    after = lax.broadcasted_iota(jnp.int32, (count, count), 1)
    rank = jnp.dot(named, (before < after).astype(jnp.float32), preferred_element_type=jnp.float32)
    place = lax.broadcasted_iota(jnp.int32, (places, clusters), 0)
    stored = (owner_lanes[...] == place // CAPACITY).astype(jnp.float32)
    named_at = jnp.dot(stored, named, preferred_element_type=jnp.float32)
    rank_at = jnp.dot(stored, rank, preferred_element_type=jnp.float32)
    turn = (lax.broadcasted_iota(jnp.int32, (places, count), 0) % CAPACITY).astype(jnp.float32)
    routing = jnp.where(rank_at == turn, named_at, 0.0).astype(jnp.bfloat16)
    lane = lax.broadcasted_iota(jnp.int32, (count, LANES), 1)
    source = lane // 64 * 64 + lane % 8 * 8 + lane // 8 % 8
    for first in range(0, width, 4 * LANES):
        pieces = []
        for start in range(first, first + 4 * LANES, LANES):
            piece = queries_ref[:, start : start + LANES].astype(jnp.float32)
            pieces.append(jnp.take_along_axis(piece, source, axis=1).astype(jnp.bfloat16))
        if first == 0:
            prefix_ref[...] = pieces[0][:, :PREFIX]
        out_ref[:, first : first + 4 * LANES] = jnp.dot(
            routing, jnp.concatenate(pieces, axis=1), preferred_element_type=jnp.float32
        ).astype(jnp.bfloat16)
    slots = jnp.zeros(lists.shape, jnp.int32)
    for cluster in range(clusters):
        slots = jnp.where(lists == cluster, owner_ref[cluster], slots)
    ranks = jnp.concatenate(
        [jnp.sum(jnp.where(name, rank, 0.0), axis=0, keepdims=True) for name in names], axis=0
    )
    target = (slots * CAPACITY).astype(jnp.float32) + ranks
    items = count * probes
    row = lax.broadcasted_iota(jnp.int32, (items, probes), 0)
    entry = lax.broadcasted_iota(jnp.int32, (items, probes), 1)
    pick = (row % probes == entry).astype(jnp.float32)
    spread = jnp.dot(pick, target, preferred_element_type=jnp.float32)
    row = lax.broadcasted_iota(jnp.int32, (items, count), 0)
    query = lax.broadcasted_iota(jnp.int32, (items, count), 1)
    target = jnp.sum(jnp.where(row // probes == query, spread, 0.0), axis=1, keepdims=True)
    place = lax.broadcasted_iota(jnp.int32, place_ref.shape, 1)
    place_ref[...] = (place == target.astype(jnp.int32)).astype(jnp.float32)


def rebuild_kernel(counts_ref, codes_ref, codebook_ref, first_ref, second_ref, table):
    fill_table(table, codebook_ref[...].T.astype(jnp.float32))

    def step(index, carry):
        first = pl.multiple_of(index * 8, 8)
        base = pl.multiple_of(index * 64, 64)
        halves = table_rows(table, base)
        for local_id, out_ref in enumerate((first_ref, second_ref)):
            for start in range(0, codes_ref.shape[2], LANES):
                codes = codes_ref[local_id, pl.ds(first, 8), start : start + LANES]
                filled = start < BLOCK * counts_ref[local_id]
                for number, tile in enumerate(looked_up(halves, codes)):
                    out_ref[pl.ds(base + number * 16, 16), start : start + LANES] = jnp.where(
                        filled, tile, jnp.zeros_like(tile)
                    )
        return carry

    lax.fori_loop(0, codes_ref.shape[1] // 8, step, 0, unroll=True)


def coarse_kernel(prefix_ref, codes_ref, codebook_ref, out_ref, table, rebuilt):
    @pl.when(pl.program_id(0) == 0)
    def _():
        fill_table(table, codebook_ref[...].astype(jnp.float32))

    halves = table_rows(table, 0)
    for start in range(0, codes_ref.shape[1], LANES):
        tiles = looked_up(halves, codes_ref[:, start : start + LANES])
        for number, tile in enumerate(tiles):
            rebuilt[number * 16 : number * 16 + 16, start : start + LANES] = tile
    out_ref[...] = jnp.dot(prefix_ref[...], rebuilt[...], preferred_element_type=jnp.float32)


def body(
    queries,
    fine_codebook,
    coarse_codebook,
    fine_codes,
    coarse_codes,
    shortlist,
    owner,
    block_counts,
):
    shards = lax.axis_size("shard")
    groups = lax.axis_size("group")
    local_count, subspaces, row_count = fine_codes.shape
    per_device, width = queries.shape[1:]
    probes = shortlist.shape[2]
    clusters = owner.shape[0]
    centers = fine_codebook.shape[0]
    slab_subspaces, slab_rows = coarse_codes.shape
    positions = clusters * CAPACITY
    queries = queries[0]
    lists = shortlist[0]

    whole = pl.BlockSpec(memory_space=pltpu.VMEM)
    outgoing, prefix, place = pl.pallas_call(
        route_kernel,
        in_specs=[whole, pl.BlockSpec(memory_space=pltpu.SMEM), whole, whole],
        out_shape=[
            jax.ShapeDtypeStruct((positions, width), jnp.bfloat16),
            jax.ShapeDtypeStruct((per_device, PREFIX), jnp.bfloat16),
            jax.ShapeDtypeStruct((per_device * probes, positions), jnp.float32),
        ],
        name="route",
    )(owner.reshape(1, clusters), owner, lists.T, queries)
    arrived = lax.all_to_all(
        outgoing.reshape(shards, positions // shards, width), "shard", 0, 0, tiled=True
    ).reshape(positions, width)

    span = CHUNK * (width // subspaces)
    rebuilt_block = pl.BlockSpec((span, row_count), lambda i: (i, 0))
    rebuilt_shape = jax.ShapeDtypeStruct((width, row_count), jnp.bfloat16)
    rebuilt = pl.pallas_call(
        rebuild_kernel,
        grid=(subspaces // CHUNK,),
        in_specs=[
            pl.BlockSpec(memory_space=pltpu.SMEM),
            pl.BlockSpec((local_count, CHUNK, row_count), lambda i: (0, i, 0)),
            pl.BlockSpec((centers, span), lambda i: (0, i)),
        ],
        out_specs=[rebuilt_block, rebuilt_block],
        out_shape=[rebuilt_shape, rebuilt_shape],
        scratch_shapes=[pltpu.VMEM((2, span, LANES), jnp.float32)],
        cost_estimate=pl.CostEstimate(
            flops=1_000_000, bytes_accessed=100_000, transcendentals=0
        ),
        name="rebuild",
    )(block_counts, fine_codes, fine_codebook)

    def from_group(value, offset):
        pairs = [((i + offset) % groups, i) for i in range(groups)]
        return lax.ppermute(value, "group", pairs)

    near = jnp.concatenate([from_group(prefix, -1), prefix, from_group(prefix, 1)], axis=0)
    around = jnp.concatenate(
        [from_group(near, -3), near, from_group(near[: 2 * per_device], 3)], axis=0
    ).reshape(groups, per_device, PREFIX)
    first = lax.axis_index("group") + groups // 2
    prefixes = jnp.roll(around, first, axis=0).reshape(groups * per_device, PREFIX)
    coarse_scores = pl.pallas_call(
        coarse_kernel,
        grid=(slab_rows // SPAN,),
        in_specs=[
            pl.BlockSpec((groups * per_device, PREFIX), lambda i: (0, 0)),
            pl.BlockSpec((slab_subspaces, SPAN), lambda i: (0, i)),
            pl.BlockSpec((PREFIX, centers), lambda i: (0, 0)),
        ],
        out_specs=pl.BlockSpec((groups * per_device, SPAN), lambda i: (0, i)),
        out_shape=jax.ShapeDtypeStruct((groups * per_device, slab_rows), jnp.float32),
        scratch_shapes=[
            pltpu.VMEM((2, PREFIX, LANES), jnp.float32),
            pltpu.VMEM((PREFIX, SPAN), jnp.bfloat16),
        ],
        cost_estimate=pl.CostEstimate(
            flops=1_000_000, bytes_accessed=100_000, transcendentals=0
        ),
        name="coarse",
    )(prefixes, coarse_codes, coarse_codebook.T)

    scores = [
        jnp.dot(arrived, columns, preferred_element_type=jnp.float32) for columns in rebuilt
    ]
    local = (jnp.arange(positions) // CAPACITY % local_count)[:, None]
    computed = jnp.where(local == 0, scores[0], scores[1])
    computed = computed.astype(jnp.bfloat16)
    returned = lax.all_to_all(
        computed.reshape(shards, positions // shards, row_count), "shard", 0, 0, tiled=True
    ).reshape(positions, row_count)
    fine_scores = jnp.dot(
        place.astype(jnp.bfloat16), returned, preferred_element_type=jnp.float32
    )
    return (
        coarse_scores.reshape(groups, per_device, slab_rows),
        fine_scores.reshape(1, per_device, probes, row_count),
    )


def solution(mesh):
    in_specs = (
        P("group", "shard", None),
        P(),
        P(),
        P("shard", None, None),
        P(None, "group"),
        P("group", "shard", None),
        P(),
        P("shard"),
    )
    out_specs = (P(None, "shard", "group"), P("group", "shard", None, None))
    return jax.shard_map(body, mesh=mesh, in_specs=in_specs, out_specs=out_specs, check_vma=False)
```
